32 devices in a mesh: parts: 2 (over x), height: 16 (over z, y, core).
Axes of the slice: x: 2, y: 2, z: 4, core: 2. Of those that a mesh axis runs over, the one named last changes fastest.
Arguments:
- snapshots: float32 [65536, 256], P(('parts', 'height')), parts along dimension 0
- fluid_mask: int32 [65536], P(('parts', 'height')), parts along dimension 0, may hold values from 0 to 1, as said below
Outputs:
- modes: float32 [32768, 256], P(('parts', 'height')), parts along dimension 0
- factor: float32 [512, 256], P('parts'), parts along dimension 0
The draws below stay inside these ranges and needn't reach their ends.
There are 2 independent parts, one for each index of `parts`. The reference program is written for one: setup_inputs(seed, part) draws one part's arguments, and reference() takes and returns one part's arrays. A program takes and returns all parts, laid end to end along the dimension named above; each array names one. Nothing has to cross between parts.
Inputs may be any that keep to these rules, and one draw needn't show every extreme that they name: `fluid_mask`: each tile of 2048 cells holds 512 to 1536 fluid cells, some tile exactly 1536; all tiles together hold exactly 16384.
All inputs are finite; a program needn't handle non-finite values.
Results may differ from the reference program's by a relative error of at most 0.0003.
Values sent between devices are 32-bit elements; how exact they have to be, the bound alone decides.
No kernel may reach another device: no remote copies, remote signals or barrier semaphores. Data moves between devices by JAX's collectives and lax.ppermute only.
A program may use at most 64 MiB of HBM per device.

```python
import jax
import jax.numpy as jnp
from jax import lax

K = 256
BLK = 1024
TILES = 16
CELLS = 2048
LOW = 512
MAXC = 1536


def shuffled_cells(key):
    return jax.random.permutation(key, CELLS)


def draw_fluid_mask(key, part):
    keys = jax.random.split(jax.random.fold_in(key, 7), 3)
    order = jax.random.permutation(keys[0], TILES)
    paired = jax.random.randint(keys[1], (TILES // 2,), LOW, MAXC + 1)
    paired = paired.at[0].set(MAXC)
    tile_counts = jnp.zeros((TILES,), jnp.int32).at[order[0::2]].set(paired).at[order[1::2]].set(2 * BLK - paired)
    ranks = jax.vmap(shuffled_cells)(jax.random.split(keys[2], TILES))
    return (ranks < tile_counts[:, None]).astype(jnp.int32).reshape(-1)


def draw_snapshots(key, part):
    row_count = TILES * CELLS
    factor_count = min(6, K // 2)
    keys = jax.random.split(jax.random.fold_in(key, 11), 8)
    tile_place = (jnp.arange(row_count) // CELLS).astype(jnp.float32)
    rising = 0.6 * jnp.exp(jnp.log(3.0) * tile_place / (TILES - 1))
    row_scale = jnp.exp(jax.random.uniform(keys[0], (row_count, 1), jnp.float32, jnp.log(0.3), jnp.log(3.0)))
    column_scale = jnp.exp(jax.random.uniform(keys[1], (1, K), jnp.float32, jnp.log(0.3), jnp.log(3.0)))
    own_level = jnp.exp(jax.random.uniform(keys[2], (K,), jnp.float32, jnp.log(0.0015), jnp.log(0.3)))
    lowest = jax.random.randint(keys[7], (), 0, K)
    own_level = own_level.at[lowest].set(0.0015)
    factor_scale = jnp.array([2.0, 1.5, 1.1, 0.8, 0.6, 0.45], jnp.float32)
    loadings = jax.random.normal(keys[3], (factor_count, K), jnp.float32)
    norm_square = jnp.zeros((K,), jnp.float32)
    for index in range(factor_count):
        loadings = loadings.at[index].multiply(factor_scale[index])
        norm_square = norm_square + loadings[index] * loadings[index]
    loadings = loadings / jnp.sqrt(norm_square + 0.05)[None, :]
    latent = jax.random.normal(keys[4], (row_count, factor_count), jnp.float32)
    apart = jax.random.normal(keys[5], (row_count, K), jnp.float32)
    values = own_level[None, :] * apart
    for index in range(factor_count):
        values = values + latent[:, index:index + 1] * loadings[index][None, :]
    return (values * column_scale * row_scale * rising[:, None]).astype(jnp.float32)


def setup_inputs(seed: int = 0, part: int = 0) -> dict:
    splits = jax.random.split(jax.random.key(seed), 3)
    part_keys = jax.random.split(jax.random.fold_in(splits[2], part), 3)
    return {
        "snapshots": draw_snapshots(jax.random.fold_in(jax.random.fold_in(splits[2], part), 71), part),
        "fluid_mask": draw_fluid_mask(jax.random.fold_in(jax.random.fold_in(splits[2], part), 71), part),
    }


highest_precision = lax.Precision.HIGHEST

def gram_matrix(row_block, row_total):
    return lax.dot_general(row_block, row_block, (((0,), (0,)), ((), ())), precision=highest_precision, preferred_element_type=jnp.float32) / row_total

def upper_factor(gram_value):
    order_size = gram_value.shape[0]
    positions = jnp.arange(order_size, dtype=jnp.int32)

    def column_step(column, lower):
        column = column.astype(jnp.int32)
        row_of = lax.dynamic_slice_in_dim(lower, column, 1, 0)[0]
        target = lax.dynamic_slice_in_dim(gram_value, column, 1, 1)[:, 0]
        residue = target - jnp.dot(lower, row_of, precision=highest_precision)
        pivot = jnp.sqrt(jnp.sum(jnp.where(positions == column, residue, 0.0)))
        entries = jnp.where(positions >= column, residue / pivot, 0.0)
        return lax.dynamic_update_slice_in_dim(lower, entries[:, None].astype(lower.dtype), column, 1)
    lower = lax.fori_loop(0, order_size, column_step, jnp.zeros_like(gram_value))
    return lower.T

def inverse_upper(factor):
    order_size = factor.shape[0]
    positions = jnp.arange(order_size, dtype=jnp.int32)

    def row_step(offset, solved):
        row = (order_size - 1 - offset).astype(jnp.int32)
        factor_row = lax.dynamic_slice_in_dim(factor, row, 1, 0)[0]
        pivot = jnp.sum(jnp.where(positions == row, factor_row, 0.0))
        unit = jnp.where(positions == row, 1.0, 0.0).astype(factor.dtype)
        entries = (unit - jnp.dot(factor_row, solved, precision=highest_precision)) / pivot
        return lax.dynamic_update_slice_in_dim(solved, entries[None, :].astype(solved.dtype), row, 0)
    return lax.fori_loop(0, order_size, row_step, jnp.zeros_like(factor))

def product(left, right):
    return jnp.dot(left, right, precision=highest_precision, preferred_element_type=jnp.float32)

def reference(snapshots, fluid_mask):
    row_total = float(TILES * BLK)
    fluid_cells = jnp.nonzero(fluid_mask > 0, size=TILES * BLK)[0]
    fluid = snapshots[fluid_cells]
    balanced = fluid.reshape(BLK, TILES, K).transpose(1, 0, 2).reshape(TILES * BLK, K)
    first_factor = upper_factor(gram_matrix(balanced, row_total))
    first_basis = product(balanced, inverse_upper(first_factor))
    second_factor = upper_factor(gram_matrix(first_basis, row_total))
    modes = product(first_basis, inverse_upper(second_factor))
    return (modes, product(second_factor, first_factor))
```

```python
import functools

import jax
import jax.numpy as jnp
from jax import lax
from jax.experimental import pallas as pl
from jax.experimental.pallas import tpu as pltpu
from jax.sharding import PartitionSpec as P

BLK = 1024
MAXC = 1536
F32 = jnp.float32
VMEM_LIMIT = 40 * 1024 * 1024


def split3(x):
    high = x.astype(jnp.bfloat16)
    rest = x - high.astype(F32)
    mid = rest.astype(jnp.bfloat16)
    return high, mid, (rest - mid.astype(F32)).astype(jnp.bfloat16)


def dot6(left, right, left_dim, right_dim):
    lh, lm, ll = split3(left)
    rh, rm, rl = split3(right)
    return lax.dot_general(
        jnp.concatenate([ll, lh, lm, lm, lh, lh], left_dim),
        jnp.concatenate([rh, rl, rm, rh, rm, rh], right_dim),
        (((left_dim,), (right_dim,)), ((), ())),
        preferred_element_type=F32,
    )


def two_sum(a, b):
    total = a + b
    part = total - a
    return total, (a - (total - part)) + (b - part)


def power_above(peak):
    power = jnp.full_like(peak, 2.0**-120)
    inverse = jnp.full_like(peak, 2.0**119)
    for step in (100, 64, 32, 16, 8, 4, 2, 1):
        trial = power * 2.0**step
        above = peak >= trial
        power = jnp.where(above, trial, power)
        inverse = jnp.where(above, inverse * 2.0**-step, inverse)
    return power * 2.0, inverse


def slices(x, bits):
    out = []
    for place in bits:
        big = 1.5 * 2.0 ** (23 - place)
        part = (x + big) - big
        out.append(part.astype(jnp.bfloat16))
        x = x - part
    part = x.astype(jnp.bfloat16)
    return out + [part, (x - part.astype(F32)).astype(jnp.bfloat16)]


def gram_pair(n1, n2, n3, n4, *n5):
    n = n1.shape[1]
    dims = (((0,), (0,)), ((), ()))
    d1 = lax.dot_general(n1, jnp.concatenate([n1, n2, n3, n4, *n5], 1), dims, preferred_element_type=F32)
    d2 = lax.dot_general(n2, jnp.concatenate([n2, n3, n4], 1), dims, preferred_element_type=F32)
    d3 = lax.dot_general(n3, n3, dims, preferred_element_type=F32)
    p11, p12, p13, p14 = (d1[:, i * n : (i + 1) * n] for i in range(4))
    p22, p23, p24 = (d2[:, i * n : (i + 1) * n] for i in range(3))
    hi, low1 = two_sum(p11, p12 + p12.T)
    hi, low2 = two_sum(hi, p22 + (p13 + p13.T))
    tail = p14 + p23 + p24
    if n5:
        tail = tail + d1[:, 4 * n :]
    return hi, (low1 + low2) + ((tail + tail.T) + d3)


def column_of(row):
    n = row.shape[1]
    return jnp.broadcast_to(row, (8, n)).T[:, 0:1]


def sweep(work, r_ref, w_ref, b=32, bi=8):
    n = work.shape[0]
    groups = b // 8
    lane = lax.broadcasted_iota(jnp.int32, (8, n), 1)
    sub_wide = lax.broadcasted_iota(jnp.int32, (8, n), 0)
    sub = lax.broadcasted_iota(jnp.int32, (8, 128), 0)

    def wide(x):
        return jnp.concatenate([x] * (n // 128), 1)

    for base in range(0, n, b):
        half = base // 128 * 128
        off = base - half
        own = (lane >= base) & (lane < base + b)
        rows, diag = [], []
        for g in range(groups):
            row = work[base + 8 * g : base + 8 * g + 8, :]
            diag.append(row[:, half : half + 128])
            rows.append(jnp.where(own, jnp.where(lane == base + 8 * g + sub_wide, 1.0, 0.0), row))
        pivots = [jnp.ones((8, 128), F32)] * groups
        for k0 in range(0, b, bi):
            col = {}
            for kk in range(bi):
                for g in range(k0 // 8, groups):
                    at = off + k0 + kk
                    col[kk, g] = jnp.broadcast_to(diag[g][:, at : at + 1], (8, 128))
            for kk in range(bi):
                own_group, s = divmod(k0 + kk, 8)
                pivot = jnp.broadcast_to(col[kk, own_group][s : s + 1, :], (8, 128))
                inverse = 1.0 / pivot
                pivots[own_group] = jnp.where(sub == s, pivot, pivots[own_group])
                mult = {}
                for g in range(own_group, groups):
                    value = col[kk, g] * inverse
                    mult[g] = jnp.where(sub > s, value, 0.0) if g == own_group else value
                for k2 in range(kk + 1, bi):
                    entry = jnp.broadcast_to(col[k2, own_group][s : s + 1, :], (8, 128))
                    for g in range(own_group, groups):
                        col[k2, g] = col[k2, g] - mult[g] * entry
                pivot_row = jnp.broadcast_to(rows[own_group][s : s + 1, :], (8, n))
                pivot_diag = jnp.broadcast_to(diag[own_group][s : s + 1, :], (8, 128))
                for g in range(own_group, groups):
                    rows[g] = rows[g] - wide(mult[g]) * pivot_row
                    diag[g] = diag[g] - mult[g] * pivot_diag
        right, full = [], []
        for g in range(groups):
            scale = lax.rsqrt(pivots[g])
            scale = scale + scale * (0.5 - (0.5 * pivots[g]) * scale * scale)
            scaled = rows[g] * wide(scale)
            own_diag = diag[g] * scale
            blocks = [own_diag if h == half else jnp.zeros((8, 128), F32) for h in range(0, n, 128)]
            upper = own & (lane >= base + 8 * g + sub_wide)
            after = jnp.where(lane >= base + b, scaled, 0.0)
            r_ref[base + 8 * g : base + 8 * g + 8, :] = jnp.where(upper, jnp.concatenate(blocks, 1), after)
            w_ref[base + 8 * g : base + 8 * g + 8, :] = jnp.where(lane < base + b, scaled, 0.0)
            right.append(after)
            full.append(scaled)
        if base + b < n:
            low = (base + b) // 128 * 128
            update = dot6(jnp.concatenate(right, 0)[:, low:], jnp.concatenate(full, 0), 0, 0)
            lanes = lax.broadcasted_iota(jnp.int32, (n - low, n), 1)
            tail = jnp.where((lanes >= base) & (lanes < base + b), 0.0, work[low:, :]) - update
            work = tail if low == 0 else jnp.concatenate([jnp.zeros((low, n), F32), tail], 0)


def block_upper(matrix, b=32):
    n = matrix.shape[0]
    row = lax.broadcasted_iota(jnp.int32, (n, n), 0) // b
    column = lax.broadcasted_iota(jnp.int32, (n, n), 1) // b
    return jnp.where(column < row, 0.0, matrix)


def gram_kernel(row_scale, x_ref, mask_ref, out_ref, a_ref, n1_ref, n2_ref, n3_ref, n4_ref):
    rows, n = x_ref.shape
    peak = jnp.zeros((1, n), F32)
    for c in range(rows // 128):
        keep = jnp.broadcast_to(mask_ref[c : c + 1, :], (128, 128)).T
        keep = jnp.concatenate([keep] * (n // 128), 1)
        chunk = jnp.where(keep > 0, x_ref[c * 128 : c * 128 + 128, :], 0.0)
        a_ref[c * 128 : c * 128 + 128, :] = chunk
        peak = jnp.maximum(peak, jnp.max(jnp.abs(chunk), axis=0, keepdims=True))
    top, shrink = power_above(peak)
    for c in range(rows // 128):
        at = slice(c * 128, c * 128 + 128)
        parts = slices(a_ref[at, :] * shrink, (6, 14, 22))
        for ref, part in zip((n1_ref, n2_ref, n3_ref, n4_ref), parts):
            ref[at, :] = part
    hi, lo = gram_pair(n1_ref[...], n2_ref[...], n3_ref[...], n4_ref[...])
    grow = top * row_scale
    column = column_of(top)
    for index, value in enumerate((hi, lo)):
        value = value * column * grow
        out_ref[index, 0:128, :] = value[0:128, 0:128]
        out_ref[index, 128:256, :] = value[0:128, 128:256]
        out_ref[index, 256:384, :] = value[128:256, 128:256]


def unpack(p):
    a, b, d = p[0:128], p[128:256], p[256:384]
    return jnp.concatenate([jnp.concatenate([a, b], 1), jnp.concatenate([b.T, d], 1)], 0)


def chain_kernel(g_ref, inv_ref, factor_ref, r1, w1, r2, w2):
    hi = unpack(g_ref[0])
    lo = unpack(g_ref[1])
    sweep(block_upper(hi), r1, w1)
    r = r1[...]
    top, shrink = power_above(jnp.max(jnp.abs(r), axis=0, keepdims=True))
    own_hi, own_lo = gram_pair(*slices(r * shrink, (7, 15, 23)))
    column = column_of(top)
    residual = (hi - own_hi * column * top) + (lo - own_lo * column * top)
    w = w1[...]
    near = dot6(w, r, 1, 1)
    gram2 = dot6(near, near, 1, 1) + dot6(dot6(w, residual, 1, 0), w, 1, 1)
    sweep(block_upper(gram2), r2, w2)
    row = lax.broadcasted_iota(jnp.int32, near.shape, 0)
    twice = jnp.where(row == lax.broadcasted_iota(jnp.int32, near.shape, 1), 2.0, 0.0)
    factor_ref[...] = dot6(r2[...], dot6(twice - near, r, 0, 0), 1, 0)
    inv_ref[...] = dot6(w2[...], w, 1, 0)


def compact_kernel(n, slots, stride, own_ref, counts_ref, mask_ref, x_ref, out_ref, rows_ref):
    shift = n.bit_length() - 1
    own = own_ref[0]
    start = lax.fori_loop(0, own, lambda s, total: total + counts_ref[s], jnp.int32(0))
    unroll = 16

    def step(block, rank):
        for u in range(unroll):
            cell = block * unroll + u
            place = ((rank + start) & (n - 1)) * stride + (rank >> shift)
            rows_ref[pl.ds(place, 1), :] = x_ref[pl.ds(cell, 1), :]
            rank = rank + mask_ref[cell]
        return rank

    lax.fori_loop(0, x_ref.shape[0] // unroll, step, jnp.int32(0))

    def copy(c, _):
        at = pl.multiple_of(c * stride, 8)
        out_ref[c] = rows_ref[pl.ds(at, slots), :]
        return 0

    lax.fori_loop(0, n, copy, 0)


def modes_kernel(n, slots, own_ref, counts_ref, recv_ref, inv_ref, out_ref, rows_ref):
    shift = n.bit_length() - 1
    own = own_ref[0]

    def place(s, start):
        first = start + ((own - start) & (n - 1))
        at = first >> shift
        turn = at & 7
        at = pl.multiple_of(at - turn, 8)
        block = pltpu.roll(jnp.concatenate([recv_ref[s], recv_ref[s, 0:8, :]], 0), turn, 0)
        head = lax.broadcasted_iota(jnp.int32, (8, block.shape[1]), 0) < turn
        rows_ref[pl.ds(at, 8), :] = jnp.where(head, rows_ref[pl.ds(at, 8), :], block[0:8])
        rows_ref[pl.ds(at + 8, slots), :] = block[8:]
        return start + counts_ref[s]

    lax.fori_loop(0, n, place, jnp.int32(0))
    out_ref[...] = dot6(rows_ref[0 : out_ref.shape[0], :], inv_ref[...], 1, 1)


VMEM = pl.BlockSpec(memory_space=pltpu.VMEM)
SMEM = pl.BlockSpec(memory_space=pltpu.SMEM)


def call(kernel, name, out, in_specs, scratch, flops, args):
    return pl.pallas_call(
        kernel,
        name=name,
        out_shape=out,
        in_specs=in_specs,
        out_specs=jax.tree.map(lambda _: VMEM, out),
        scratch_shapes=scratch,
        compiler_params=pltpu.CompilerParams(vmem_limit_bytes=VMEM_LIMIT),
        cost_estimate=pl.CostEstimate(flops=flops, bytes_accessed=4 << 20, transcendentals=0),
    )(*args)


def reduce_pair(pair, n, own):
    def other(x, bit):
        return lax.ppermute(x, "height", [(i, i ^ bit) for i in range(n)])

    def add(a, b):
        total, error = two_sum(a[0], b[0])
        return jnp.stack([total, (a[1] + b[1]) + error])

    halved = [1, 2]
    for bit in halved:
        size = pair.shape[1] // 2
        mine = jnp.where((own & bit) > 0, size, 0)
        sent = lax.dynamic_slice_in_dim(pair, size - mine, size, 1)
        pair = add(lax.dynamic_slice_in_dim(pair, mine, size, 1), other(sent, bit))
    bit = 4
    while bit < n:
        pair = add(pair, other(pair, bit))
        bit *= 2
    for bit in halved[::-1]:
        got = other(pair, bit)
        high = (own & bit) > 0
        pair = jnp.concatenate([jnp.where(high, got, pair), jnp.where(high, pair, got)], 1)
    return pair


def local(snapshots, fluid_mask):
    n = lax.axis_size("height")
    own = lax.axis_index("height")
    cells, k = snapshots.shape
    slots = (-(-MAXC // n) + 7) // 8 * 8
    stride = slots + 8
    own_list = own.reshape(1)

    pair = call(
        functools.partial(gram_kernel, 1.0 / (n * BLK)),
        "gram",
        jax.ShapeDtypeStruct((2, 384, 128), F32),
        [VMEM, VMEM],
        [pltpu.VMEM((cells, k), F32)] + [pltpu.VMEM((cells, k), jnp.bfloat16)] * 4,
        16 * cells * k * k,
        (snapshots, fluid_mask.reshape(cells // 128, 128)),
    )
    counts = jnp.where(jnp.arange(n) == own, jnp.sum(fluid_mask), 0)
    bit = 1
    while bit < n:
        counts = counts + lax.ppermute(counts, "height", [(i, i ^ bit) for i in range(n)])
        bit *= 2
    outgoing = call(
        functools.partial(compact_kernel, n, slots, stride),
        "compact",
        jax.ShapeDtypeStruct((n, slots, k), F32),
        [SMEM, SMEM, SMEM, VMEM],
        [pltpu.VMEM((n * stride, k), F32)],
        1 << 30,
        (own_list, counts, fluid_mask, snapshots),
    )
    received = lax.all_to_all(outgoing, "height", split_axis=0, concat_axis=0, tiled=True)
    pair = reduce_pair(pair, n, own)
    square = jax.ShapeDtypeStruct((k, k), F32)
    inverse, factor = call(
        chain_kernel,
        "chain",
        [square, square],
        [VMEM],
        [pltpu.VMEM((k, k), F32)] * 4,
        20 << 30,
        (pair,),
    )
    modes = call(
        functools.partial(modes_kernel, n, slots),
        "modes",
        jax.ShapeDtypeStruct((BLK, k), F32),
        [SMEM, SMEM, VMEM, VMEM],
        [pltpu.VMEM((BLK + slots + 8, k), F32)],
        12 * BLK * k * k,
        (own_list, counts, received, inverse),
    )
    return (modes, factor)


def solution(mesh):
    return jax.shard_map(
        local,
        mesh=mesh,
        in_specs=(P(("parts", "height"), None), P(("parts", "height"))),
        out_specs=(P(("parts", "height"), None), P("parts", None)),
        check_vma=False,
    )
```

```python
import functools

import jax
import jax.numpy as jnp
from jax import lax
from jax.experimental import pallas as pl
from jax.experimental.pallas import tpu as pltpu
from jax.sharding import PartitionSpec as P

BLK = 1024
MAXC = 1536
F32 = jnp.float32
VMEM_LIMIT = 40 * 1024 * 1024


def split3(x):
    high = x.astype(jnp.bfloat16)
    rest = x - high.astype(F32)
    mid = rest.astype(jnp.bfloat16)
    return high, mid, (rest - mid.astype(F32)).astype(jnp.bfloat16)


def dot6(left, right, left_dim, right_dim):
    lh, lm, ll = split3(left)
    rh, rm, rl = split3(right)
    return lax.dot_general(
        jnp.concatenate([ll, lh, lm, lm, lh, lh], left_dim),
        jnp.concatenate([rh, rl, rm, rh, rm, rh], right_dim),
        (((left_dim,), (right_dim,)), ((), ())),
        preferred_element_type=F32,
    )


def two_sum(a, b):
    total = a + b
    part = total - a
    return total, (a - (total - part)) + (b - part)


def add_pair(a, b):
    total, error = two_sum(a[0], b[0])
    return total, (a[1] + b[1]) + error


def power_above(peak):
    power = jnp.full_like(peak, 2.0**-120)
    inverse = jnp.full_like(peak, 2.0**119)
    for step in (100, 64, 32, 16, 8, 4, 2, 1):
        trial = power * 2.0**step
        above = peak >= trial
        power = jnp.where(above, trial, power)
        inverse = jnp.where(above, inverse * 2.0**-step, inverse)
    return power * 2.0, inverse


def slices(x, bits):
    out = []
    for place in bits:
        big = 1.5 * 2.0 ** (23 - place)
        part = (x + big) - big
        out.append(part.astype(jnp.bfloat16))
        x = x - part
    part = x.astype(jnp.bfloat16)
    return out + [part, (x - part.astype(F32)).astype(jnp.bfloat16)]


def gram_pair(n1, n2, n3, n4, *n5):
    n = n1.shape[1]
    dims = (((0,), (0,)), ((), ()))
    d1 = lax.dot_general(n1, jnp.concatenate([n1, n2, n3, n4, *n5], 1), dims, preferred_element_type=F32)
    d2 = lax.dot_general(n2, jnp.concatenate([n2, n3, n4], 1), dims, preferred_element_type=F32)
    d3 = lax.dot_general(n3, n3, dims, preferred_element_type=F32)
    p11, p12, p13, p14 = (d1[:, i * n : (i + 1) * n] for i in range(4))
    p22, p23, p24 = (d2[:, i * n : (i + 1) * n] for i in range(3))
    hi, low1 = two_sum(p11, p12 + p12.T)
    hi, low2 = two_sum(hi, p22 + (p13 + p13.T))
    tail = p14 + p23 + p24
    if n5:
        tail = tail + d1[:, 4 * n :]
    return hi, (low1 + low2) + ((tail + tail.T) + d3)


def column_of(row):
    n = row.shape[1]
    return jnp.broadcast_to(row, (8, n)).T[:, 0:1]


def sweep(work, r_ref, w_ref, b=32, bi=8):
    n = work.shape[0]
    groups = b // 8
    lane = lax.broadcasted_iota(jnp.int32, (8, n), 1)
    sub_wide = lax.broadcasted_iota(jnp.int32, (8, n), 0)
    sub = lax.broadcasted_iota(jnp.int32, (8, 128), 0)

    def wide(x):
        return jnp.concatenate([x] * (n // 128), 1)

    for base in range(0, n, b):
        half = base // 128 * 128
        off = base - half
        own = (lane >= base) & (lane < base + b)
        rows, diag = [], []
        for g in range(groups):
            row = work[base + 8 * g : base + 8 * g + 8, :]
            diag.append(row[:, half : half + 128])
            rows.append(jnp.where(own, jnp.where(lane == base + 8 * g + sub_wide, 1.0, 0.0), row))
        pivots = [jnp.ones((8, 128), F32)] * groups
        for k0 in range(0, b, bi):
            col = {}
            for kk in range(bi):
                for g in range(k0 // 8, groups):
                    at = off + k0 + kk
                    col[kk, g] = jnp.broadcast_to(diag[g][:, at : at + 1], (8, 128))
            for kk in range(bi):
                own_group, s = divmod(k0 + kk, 8)
                pivot = jnp.broadcast_to(col[kk, own_group][s : s + 1, :], (8, 128))
                inverse = 1.0 / pivot
                pivots[own_group] = jnp.where(sub == s, pivot, pivots[own_group])
                mult = {}
                for g in range(own_group, groups):
                    value = col[kk, g] * inverse
                    mult[g] = jnp.where(sub > s, value, 0.0) if g == own_group else value
                for k2 in range(kk + 1, bi):
                    entry = jnp.broadcast_to(col[k2, own_group][s : s + 1, :], (8, 128))
                    for g in range(own_group, groups):
                        col[k2, g] = col[k2, g] - mult[g] * entry
                pivot_row = jnp.broadcast_to(rows[own_group][s : s + 1, :], (8, n))
                pivot_diag = jnp.broadcast_to(diag[own_group][s : s + 1, :], (8, 128))
                for g in range(own_group, groups):
                    rows[g] = rows[g] - wide(mult[g]) * pivot_row
                    diag[g] = diag[g] - mult[g] * pivot_diag
        right, full = [], []
        for g in range(groups):
            scale = lax.rsqrt(pivots[g])
            scale = scale + scale * (0.5 - (0.5 * pivots[g]) * scale * scale)
            scaled = rows[g] * wide(scale)
            own_diag = diag[g] * scale
            blocks = [own_diag if h == half else jnp.zeros((8, 128), F32) for h in range(0, n, 128)]
            upper = own & (lane >= base + 8 * g + sub_wide)
            after = jnp.where(lane >= base + b, scaled, 0.0)
            r_ref[base + 8 * g : base + 8 * g + 8, :] = jnp.where(upper, jnp.concatenate(blocks, 1), after)
            w_ref[base + 8 * g : base + 8 * g + 8, :] = jnp.where(lane < base + b, scaled, 0.0)
            right.append(after)
            full.append(scaled)
        if base + b < n:
            low = (base + b) // 128 * 128
            update = dot6(jnp.concatenate(right, 0)[:, low:], jnp.concatenate(full, 0), 0, 0)
            lanes = lax.broadcasted_iota(jnp.int32, (n - low, n), 1)
            tail = jnp.where((lanes >= base) & (lanes < base + b), 0.0, work[low:, :]) - update
            work = tail if low == 0 else jnp.concatenate([jnp.zeros((low, n), F32), tail], 0)


def block_upper(matrix, b=32):
    n = matrix.shape[0]
    row = lax.broadcasted_iota(jnp.int32, (n, n), 0) // b
    column = lax.broadcasted_iota(jnp.int32, (n, n), 1) // b
    return jnp.where(column < row, 0.0, matrix)


def gram_kernel(row_scale, own_ref, x_ref, mask_ref, keep_ref, send_ref, a_ref, n1_ref, n2_ref, n3_ref, n4_ref):
    rows, n = x_ref.shape
    peak = jnp.zeros((8, n), F32)
    for c in range(rows // 128):
        keep = jnp.broadcast_to(mask_ref[c : c + 1, :], (128, 128)).T
        keep = jnp.concatenate([keep] * (n // 128), 1)
        chunk = jnp.where(keep > 0, x_ref[c * 128 : c * 128 + 128, :], 0.0)
        a_ref[c * 128 : c * 128 + 128, :] = chunk
        peak = jnp.maximum(peak, jnp.max(jnp.abs(chunk).reshape(16, 8, n), axis=0))
    top, shrink = power_above(jnp.max(peak, axis=0, keepdims=True))
    for c in range(rows // 128):
        at = slice(c * 128, c * 128 + 128)
        for ref, part in zip((n1_ref, n2_ref, n3_ref, n4_ref), slices(a_ref[at, :] * shrink, (6, 14, 22))):
            ref[at, :] = part
    pair = gram_pair(n1_ref[...], n2_ref[...], n3_ref[...], n4_ref[...])
    column, grow = column_of(top), top * row_scale
    odd = (own_ref[0] & 1) > 0
    live = jnp.sum(mask_ref[...].astype(F32), axis=(0, 1), keepdims=True)
    lane = lax.broadcasted_iota(jnp.int32, (8, 128), 1)
    count = jnp.where(lane == own_ref[0], live, 0.0)
    for index, value in enumerate(pair):
        value = value * column * grow
        blocks = (value[0:128, 0:128], value[0:128, 128:256], value[128:256, 128:256])
        first = jnp.concatenate([blocks[0], blocks[1][0:64]], 0)
        second = jnp.concatenate([blocks[1][64:128], blocks[2]], 0)
        size = first.shape[0]
        keep_ref[index, 0:size] = jnp.where(odd, second, first)
        send_ref[index, 0:size] = jnp.where(odd, first, second)
        for ref in (keep_ref, send_ref):
            ref[index, size:] = count if index == 0 else jnp.zeros_like(count)


def quarter_kernel(own_ref, keep_ref, got_ref, mine_ref, *send_refs):
    size = mine_ref.shape[1] - 8
    place = (own_ref[0] >> 1) & 3
    for turn, ref in enumerate((mine_ref,) + send_refs):
        for to, at in (
            (pl.ds(0, size), pl.ds(pl.multiple_of((place ^ turn) * size, 8), size)),
            (pl.ds(size, 8), pl.ds(4 * size, 8)),
        ):
            ref[0, to, :], ref[1, to, :] = add_pair(
                (keep_ref[0, at, :], keep_ref[1, at, :]), (got_ref[0, at, :], got_ref[1, at, :])
            )


def unpack(p):
    a, b, d = p[0:128], p[128:256], p[256:384]
    return jnp.concatenate([jnp.concatenate([a, b], 1), jnp.concatenate([b.T, d], 1)], 0)


def chain_kernel(own_ref, half_ref, got_ref, inv_ref, factor_ref, r1, w1, r2, w2):
    odd = (own_ref[0] & 1) > 0
    hi, lo = (
        unpack(jnp.concatenate([jnp.where(odd, got, half), jnp.where(odd, half, got)], 0))
        for half, got in ((half_ref[0], got_ref[0]), (half_ref[1], got_ref[1]))
    )
    sweep(block_upper(hi), r1, w1)
    r = r1[...]
    top, shrink = power_above(jnp.max(jnp.abs(r), axis=0, keepdims=True))
    own_hi, own_lo = gram_pair(*slices(r * shrink, (7, 15, 23)))
    column = column_of(top)
    residual = (hi - own_hi * column * top) + (lo - own_lo * column * top)
    w = w1[...]
    near = dot6(w, r, 1, 1)
    gram2 = dot6(near, near, 1, 1) + dot6(dot6(w, residual, 1, 0), w, 1, 1)
    sweep(block_upper(gram2), r2, w2)
    row = lax.broadcasted_iota(jnp.int32, near.shape, 0)
    twice = jnp.where(row == lax.broadcasted_iota(jnp.int32, near.shape, 1), 2.0, 0.0)
    factor_ref[...] = dot6(r2[...], dot6(twice - near, r, 0, 0), 1, 0)
    inv_ref[...] = dot6(w2[...], w, 1, 0)


def compact_kernel(n, starts_ref, mask_ref, x_ref, out_ref, rank_ref):
    slots = out_ref.shape[1]
    shift = n.bit_length() - 1
    width = 16
    blocks = mask_ref.shape[0]
    live = mask_ref[...]
    before = lax.broadcasted_iota(jnp.int32, (128, 128), 0) < lax.broadcasted_iota(jnp.int32, (128, 128), 1)
    rank_ref[...] = jnp.dot(
        live.astype(F32).astype(jnp.bfloat16),
        jnp.where(before, 1.0, 0.0).astype(jnp.bfloat16),
        preferred_element_type=F32,
    ).astype(jnp.int32)
    out_ref[...] = jnp.zeros_like(out_ref)
    row = lax.broadcasted_iota(jnp.int32, (n * width, 128), 0)

    def step(b, _):
        first = starts_ref[b]
        low = pl.multiple_of(jnp.minimum((first >> shift) & -8, slots - width), 8)
        rank = rank_ref[pl.ds(b, 1), :] + first
        target = (rank & (n - 1)) * width + (rank >> shift) - low
        target = jnp.where(mask_ref[pl.ds(b, 1), :] > 0, target, -1)
        pick = jnp.where(row == target, 1.0, 0.0).astype(jnp.bfloat16)
        cells = x_ref[pl.ds(pl.multiple_of(b * 128, 128), 128), :]
        moved = jnp.dot(
            jnp.concatenate([pick] * 3, 1), jnp.concatenate(split3(cells), 0), preferred_element_type=F32
        )
        for c in range(n):
            out_ref[c, pl.ds(low, width), :] += moved[c * width : c * width + width]
        return 0

    lax.fori_loop(0, blocks, step, 0, unroll=4 if n <= 16 else 1)


def turn_kernel(n, own_ref, counts_ref, blocks_ref, out_ref, sem):
    start = lax.fori_loop(0, own_ref[0], lambda s, total: total + counts_ref[s], jnp.int32(0))
    copies = [
        pltpu.make_async_copy(blocks_ref.at[(d - start) & (n - 1)], out_ref.at[d], sem.at[d]) for d in range(n)
    ]
    for copy in copies:
        copy.start()
    for copy in copies:
        copy.wait()


def modes_kernel(n, slots, own_ref, counts_ref, recv_ref, inv_ref, out_ref, rows_ref, done_ref, sem):
    shift = n.bit_length() - 1
    own = own_ref[0]

    def place(s, start):
        first = start + ((own - start) & (n - 1))
        at = first >> shift
        turn = at & 7
        at = pl.multiple_of(at - turn, 8)
        block = pltpu.roll(jnp.concatenate([recv_ref[s], recv_ref[s, 0:8, :]], 0), turn, 0)
        head = lax.broadcasted_iota(jnp.int32, (8, block.shape[1]), 0) < turn
        rows_ref[pl.ds(at, 8), :] = jnp.where(head, rows_ref[pl.ds(at, 8), :], block[0:8])
        rows_ref[pl.ds(at + 8, slots), :] = block[8:]
        return start + counts_ref[s]

    lax.fori_loop(0, n, place, jnp.int32(0))
    step = out_ref.shape[0] // sem.shape[0]
    copies = []
    for c in range(sem.shape[0]):
        at = pl.ds(c * step, step)
        done_ref[at, :] = dot6(rows_ref[at, :], inv_ref[...], 1, 1)
        copies.append(pltpu.make_async_copy(done_ref.at[at], out_ref.at[at], sem.at[c]))
        copies[-1].start()
    for copy in copies:
        copy.wait()


VMEM = pl.BlockSpec(memory_space=pltpu.VMEM)
SMEM = pl.BlockSpec(memory_space=pltpu.SMEM)
HBM = pl.BlockSpec(memory_space=pltpu.HBM)


def call(kernel, name, out, in_specs, scratch, flops, args, out_space=VMEM):
    return pl.pallas_call(
        kernel,
        name=name,
        out_shape=out,
        in_specs=in_specs,
        out_specs=jax.tree.map(lambda _: out_space, out),
        scratch_shapes=scratch,
        compiler_params=pltpu.CompilerParams(vmem_limit_bytes=VMEM_LIMIT),
        cost_estimate=pl.CostEstimate(flops=flops, bytes_accessed=4 << 20, transcendentals=0),
    )(*args)


def other(x, bits, n):
    return lax.ppermute(x, "height", [(i, i ^ bits) for i in range(n)])


def add(a, b):
    return jnp.stack(add_pair(a, b))


def gather_quarters(mine, n):
    return [mine] + [other(mine, 2 * turn, n) for turn in (3, 2, 1)][::-1]


def assemble(got, own):
    place = (own >> 1) & 3
    return jnp.concatenate(
        [
            jnp.where(place < 2, *(jnp.where((place & 1) > 0, got[c ^ h ^ 1], got[c ^ h]) for h in (0, 2)))
            for c in range(4)
        ],
        1,
    )


def local(snapshots, fluid_mask):
    n = lax.axis_size("height")
    own = lax.axis_index("height")
    cells, k = snapshots.shape
    slots = (-(-MAXC // n) + 7) // 8 * 8
    own_list = own.reshape(1)
    mask = fluid_mask.reshape(cells // 128, 128)
    block = jnp.arange(cells // 128)
    starts = jnp.sum(jnp.where(block[None, :, None] < block[:, None, None], mask[None], 0), (1, 2))
    half = jax.ShapeDtypeStruct((2, 200, 128), F32)
    keep, send = call(
        functools.partial(gram_kernel, 1.0 / (n * BLK)),
        "gram",
        [half, half],
        [SMEM, VMEM, VMEM],
        [pltpu.VMEM((cells, k), F32)] + [pltpu.VMEM((cells, k), jnp.bfloat16)] * 4,
        16 * cells * k * k,
        (own_list, snapshots, mask),
    )
    size = keep.shape[1] // 4 // 8 * 8
    quarter = jax.ShapeDtypeStruct((2, size + 8, 128), F32)
    mine, side, up, across = call(
        quarter_kernel, "quarter", [quarter] * 4, [SMEM, VMEM, VMEM], [], 1 << 20, (own_list, keep, other(send, 1, n))
    )
    got = [other(across, 6, n), other(up, 4, n), other(side, 2, n)]
    starts, mine = lax.optimization_barrier((starts, mine))
    blocks = call(
        functools.partial(compact_kernel, n),
        "compact",
        jax.ShapeDtypeStruct((n, slots, k), F32),
        [SMEM, VMEM, VMEM],
        [pltpu.VMEM((cells // 128, 128), jnp.int32)],
        4 << 30,
        (starts, mask, snapshots),
    )
    got, blocks = lax.optimization_barrier((got, blocks))
    mine = add(add(mine, got[0]), add(got[1], got[2]))
    bit = 8
    while bit < n:
        mine = add(mine, other(mine, bit, n))
        bit *= 2
    counts = mine[0, size, :n].astype(jnp.int32)
    quarters = gather_quarters(mine[:, :size], n)
    outgoing = call(
        functools.partial(turn_kernel, n),
        "turn",
        jax.ShapeDtypeStruct((n, slots, k), F32),
        [SMEM, SMEM, VMEM],
        [pltpu.SemaphoreType.DMA((n,))],
        1 << 20,
        (own_list, counts, blocks),
        out_space=HBM,
    )
    quarters, outgoing = lax.optimization_barrier((quarters, outgoing))
    received = lax.all_to_all(outgoing, "height", split_axis=0, concat_axis=0, tiled=True)
    half = assemble(quarters, own)
    got = other(half, 1, n)
    square = jax.ShapeDtypeStruct((k, k), F32)
    inverse, factor = call(
        chain_kernel,
        "chain",
        [square, square],
        [SMEM, VMEM, VMEM],
        [pltpu.VMEM((k, k), F32)] * 4,
        20 << 30,
        (own_list, half, got),
    )
    modes = call(
        functools.partial(modes_kernel, n, slots),
        "modes",
        jax.ShapeDtypeStruct((BLK, k), F32),
        [SMEM, SMEM, VMEM, VMEM],
        [pltpu.VMEM((BLK + slots + 8, k), F32), pltpu.VMEM((BLK, k), F32), pltpu.SemaphoreType.DMA((4,))],
        12 * BLK * k * k,
        (own_list, counts, received, inverse),
        out_space=HBM,
    )
    return (modes, factor)


def solution(mesh):
    return jax.shard_map(
        local,
        mesh=mesh,
        in_specs=(P(("parts", "height"), None), P(("parts", "height"))),
        out_specs=(P(("parts", "height"), None), P("parts", None)),
        check_vma=False,
    )
```

```python
import functools

import jax
import jax.numpy as jnp
from jax import lax
from jax.experimental import pallas as pl
from jax.experimental.pallas import tpu as pltpu
from jax.sharding import PartitionSpec as P

BLK = 1024
MAXC = 1536
F32 = jnp.float32
VMEM_LIMIT = 40 * 1024 * 1024


def split3(x):
    high = x.astype(jnp.bfloat16)
    rest = x - high.astype(F32)
    mid = rest.astype(jnp.bfloat16)
    return high, mid, (rest - mid.astype(F32)).astype(jnp.bfloat16)


def dot6(left, right, left_dim, right_dim):
    lh, lm, ll = split3(left)
    rh, rm, rl = split3(right)
    return lax.dot_general(
        jnp.concatenate([ll, lh, lm, lm, lh, lh], left_dim),
        jnp.concatenate([rh, rl, rm, rh, rm, rh], right_dim),
        (((left_dim,), (right_dim,)), ((), ())),
        preferred_element_type=F32,
    )


def two_sum(a, b):
    total = a + b
    part = total - a
    return total, (a - (total - part)) + (b - part)


def add_pair(a, b):
    total, error = two_sum(a[0], b[0])
    return total, (a[1] + b[1]) + error


def power_above(peak):
    power = jnp.full_like(peak, 2.0**-120)
    inverse = jnp.full_like(peak, 2.0**119)
    for step in (100, 64, 32, 16, 8, 4, 2, 1):
        trial = power * 2.0**step
        above = peak >= trial
        power = jnp.where(above, trial, power)
        inverse = jnp.where(above, inverse * 2.0**-step, inverse)
    return power * 2.0, inverse


def slices(x, bits):
    out = []
    for place in bits:
        big = 1.5 * 2.0 ** (23 - place)
        part = (x + big) - big
        out.append(part.astype(jnp.bfloat16))
        x = x - part
    part = x.astype(jnp.bfloat16)
    return out + [part, (x - part.astype(F32)).astype(jnp.bfloat16)]


def gram_pair(n1, n2, n3, n4, *n5):
    n = n1.shape[1]
    dims = (((0,), (0,)), ((), ()))
    d1 = lax.dot_general(n1, jnp.concatenate([n1, n2, n3, n4, *n5], 1), dims, preferred_element_type=F32)
    d2 = lax.dot_general(n2, jnp.concatenate([n2, n3, n4], 1), dims, preferred_element_type=F32)
    d3 = lax.dot_general(n3, n3, dims, preferred_element_type=F32)
    p11, p12, p13, p14 = (d1[:, i * n : (i + 1) * n] for i in range(4))
    p22, p23, p24 = (d2[:, i * n : (i + 1) * n] for i in range(3))
    hi, low1 = two_sum(p11, p12 + p12.T)
    hi, low2 = two_sum(hi, p22 + (p13 + p13.T))
    tail = p14 + p23 + p24
    if n5:
        tail = tail + d1[:, 4 * n :]
    return hi, (low1 + low2) + ((tail + tail.T) + d3)


def column_of(row):
    n = row.shape[1]
    return jnp.broadcast_to(row, (8, n)).T[:, 0:1]


def sweep(work, r_ref, w_ref, b=32, bi=8):
    n = work.shape[0]
    groups = b // 8
    lane = lax.broadcasted_iota(jnp.int32, (8, n), 1)
    sub_wide = lax.broadcasted_iota(jnp.int32, (8, n), 0)
    sub = lax.broadcasted_iota(jnp.int32, (8, 128), 0)

    def wide(x):
        return jnp.concatenate([x] * (n // 128), 1)

    for base in range(0, n, b):
        half = base // 128 * 128
        off = base - half
        own = (lane >= base) & (lane < base + b)
        rows, diag = [], []
        for g in range(groups):
            row = work[base + 8 * g : base + 8 * g + 8, :]
            diag.append(row[:, half : half + 128])
            rows.append(jnp.where(own, jnp.where(lane == base + 8 * g + sub_wide, 1.0, 0.0), row))
        pivots = [jnp.ones((8, 128), F32)] * groups
        for k0 in range(0, b, bi):
            col = {}
            for kk in range(bi):
                for g in range(k0 // 8, groups):
                    at = off + k0 + kk
                    col[kk, g] = jnp.broadcast_to(diag[g][:, at : at + 1], (8, 128))
            for kk in range(bi):
                own_group, s = divmod(k0 + kk, 8)
                pivot = jnp.broadcast_to(col[kk, own_group][s : s + 1, :], (8, 128))
                inverse = 1.0 / pivot
                pivots[own_group] = jnp.where(sub == s, pivot, pivots[own_group])
                mult = {}
                for g in range(own_group, groups):
                    value = col[kk, g] * inverse
                    mult[g] = jnp.where(sub > s, value, 0.0) if g == own_group else value
                for k2 in range(kk + 1, bi):
                    entry = jnp.broadcast_to(col[k2, own_group][s : s + 1, :], (8, 128))
                    for g in range(own_group, groups):
                        col[k2, g] = col[k2, g] - mult[g] * entry
                pivot_row = jnp.broadcast_to(rows[own_group][s : s + 1, :], (8, n))
                pivot_diag = jnp.broadcast_to(diag[own_group][s : s + 1, :], (8, 128))
                for g in range(own_group, groups):
                    rows[g] = rows[g] - wide(mult[g]) * pivot_row
                    diag[g] = diag[g] - mult[g] * pivot_diag
        right, full = [], []
        for g in range(groups):
            scale = lax.rsqrt(pivots[g])
            scale = scale + scale * (0.5 - (0.5 * pivots[g]) * scale * scale)
            scaled = rows[g] * wide(scale)
            own_diag = diag[g] * scale
            blocks = [own_diag if h == half else jnp.zeros((8, 128), F32) for h in range(0, n, 128)]
            upper = own & (lane >= base + 8 * g + sub_wide)
            after = jnp.where(lane >= base + b, scaled, 0.0)
            r_ref[base + 8 * g : base + 8 * g + 8, :] = jnp.where(upper, jnp.concatenate(blocks, 1), after)
            w_ref[base + 8 * g : base + 8 * g + 8, :] = jnp.where(lane < base + b, scaled, 0.0)
            right.append(after)
            full.append(scaled)
        if base + b < n:
            low = (base + b) // 128 * 128
            update = dot6(jnp.concatenate(right, 0)[:, low:], jnp.concatenate(full, 0), 0, 0)
            lanes = lax.broadcasted_iota(jnp.int32, (n - low, n), 1)
            tail = jnp.where((lanes >= base) & (lanes < base + b), 0.0, work[low:, :]) - update
            work = tail if low == 0 else jnp.concatenate([jnp.zeros((low, n), F32), tail], 0)


def block_upper(matrix, b=32):
    n = matrix.shape[0]
    row = lax.broadcasted_iota(jnp.int32, (n, n), 0) // b
    column = lax.broadcasted_iota(jnp.int32, (n, n), 1) // b
    return jnp.where(column < row, 0.0, matrix)


def gram_kernel(row_scale, own_ref, x_ref, mask_ref, keep_ref, send_ref, a_ref, n1_ref, n2_ref, n3_ref, n4_ref):
    rows, n = x_ref.shape
    peak = jnp.zeros((8, n), F32)
    for c in range(rows // 128):
        keep = jnp.broadcast_to(mask_ref[c : c + 1, :], (128, 128)).T
        keep = jnp.concatenate([keep] * (n // 128), 1)
        chunk = jnp.where(keep > 0, x_ref[c * 128 : c * 128 + 128, :], 0.0)
        a_ref[c * 128 : c * 128 + 128, :] = chunk
        peak = jnp.maximum(peak, jnp.max(jnp.abs(chunk).reshape(16, 8, n), axis=0))
    top, shrink = power_above(jnp.max(peak, axis=0, keepdims=True))
    for c in range(rows // 128):
        at = slice(c * 128, c * 128 + 128)
        for ref, part in zip((n1_ref, n2_ref, n3_ref, n4_ref), slices(a_ref[at, :] * shrink, (6, 14, 22))):
            ref[at, :] = part
    pair = gram_pair(n1_ref[...], n2_ref[...], n3_ref[...], n4_ref[...])
    column, grow = column_of(top), top * row_scale
    odd = (own_ref[0] & 1) > 0
    live = jnp.sum(mask_ref[...].astype(F32), axis=(0, 1), keepdims=True)
    lane = lax.broadcasted_iota(jnp.int32, (8, 128), 1)
    count = jnp.where(lane == own_ref[0], live, 0.0)
    for index, value in enumerate(pair):
        value = value * column * grow
        blocks = (value[0:128, 0:128], value[0:128, 128:256], value[128:256, 128:256])
        first = jnp.concatenate([blocks[0], blocks[1][0:64]], 0)
        second = jnp.concatenate([blocks[1][64:128], blocks[2]], 0)
        size = first.shape[0]
        keep_ref[index, 0:size] = jnp.where(odd, second, first)
        send_ref[index, 0:size] = jnp.where(odd, first, second)
        for ref in (keep_ref, send_ref):
            ref[index, size:] = count if index == 0 else jnp.zeros_like(count)


def quarter_kernel(own_ref, keep_ref, got_ref, mine_ref, *send_refs):
    size = mine_ref.shape[1] - 8
    place = (own_ref[0] >> 1) & 3
    for turn, ref in enumerate((mine_ref,) + send_refs):
        for to, at in (
            (pl.ds(0, size), pl.ds(pl.multiple_of((place ^ turn) * size, 8), size)),
            (pl.ds(size, 8), pl.ds(4 * size, 8)),
        ):
            ref[0, to, :], ref[1, to, :] = add_pair(
                (keep_ref[0, at, :], keep_ref[1, at, :]), (got_ref[0, at, :], got_ref[1, at, :])
            )


def unpack(p):
    a, b, d = p[0:128], p[128:256], p[256:384]
    return jnp.concatenate([jnp.concatenate([a, b], 1), jnp.concatenate([b.T, d], 1)], 0)


def chain_kernel(own_ref, half_ref, got_ref, inv_ref, factor_ref, r1, w1, r2, w2):
    odd = (own_ref[0] & 1) > 0
    hi, lo = (
        unpack(jnp.concatenate([jnp.where(odd, got, half), jnp.where(odd, half, got)], 0))
        for half, got in ((half_ref[0], got_ref[0]), (half_ref[1], got_ref[1]))
    )
    sweep(block_upper(hi), r1, w1)
    r = r1[...]
    top, shrink = power_above(jnp.max(jnp.abs(r), axis=0, keepdims=True))
    own_hi, own_lo = gram_pair(*slices(r * shrink, (7, 15, 23)))
    column = column_of(top)
    residual = (hi - own_hi * column * top) + (lo - own_lo * column * top)
    w = w1[...]
    near = dot6(w, r, 1, 1)
    gram2 = dot6(near, near, 1, 1) + dot6(dot6(w, residual, 1, 0), w, 1, 1)
    sweep(block_upper(gram2), r2, w2)
    row = lax.broadcasted_iota(jnp.int32, near.shape, 0)
    twice = jnp.where(row == lax.broadcasted_iota(jnp.int32, near.shape, 1), 2.0, 0.0)
    factor_ref[...] = dot6(r2[...], dot6(twice - near, r, 0, 0), 1, 0)
    inv_ref[...] = dot6(w2[...], w, 1, 0)


def compact_kernel(n, starts_ref, mask_ref, x_ref, out_ref, rank_ref):
    slots = out_ref.shape[1]
    shift = n.bit_length() - 1
    width = 16
    blocks = mask_ref.shape[0]
    live = mask_ref[...]
    before = lax.broadcasted_iota(jnp.int32, (128, 128), 0) < lax.broadcasted_iota(jnp.int32, (128, 128), 1)
    rank_ref[...] = jnp.dot(
        live.astype(F32).astype(jnp.bfloat16),
        jnp.where(before, 1.0, 0.0).astype(jnp.bfloat16),
        preferred_element_type=F32,
    ).astype(jnp.int32)
    out_ref[...] = jnp.zeros_like(out_ref)
    row = lax.broadcasted_iota(jnp.int32, (n * width, 128), 0)

    def step(b, _):
        first = starts_ref[b]
        low = pl.multiple_of(jnp.minimum((first >> shift) & -8, slots - width), 8)
        rank = rank_ref[pl.ds(b, 1), :] + first
        target = (rank & (n - 1)) * width + (rank >> shift) - low
        target = jnp.where(mask_ref[pl.ds(b, 1), :] > 0, target, -1)
        pick = jnp.where(row == target, 1.0, 0.0).astype(jnp.bfloat16)
        cells = x_ref[pl.ds(pl.multiple_of(b * 128, 128), 128), :]
        moved = jnp.dot(
            jnp.concatenate([pick] * 3, 1), jnp.concatenate(split3(cells), 0), preferred_element_type=F32
        )
        for c in range(n):
            out_ref[c, pl.ds(low, width), :] += moved[c * width : c * width + width]
        return 0

    lax.fori_loop(0, blocks, step, 0, unroll=4 if n <= 16 else 1)


def turn_kernel(n, own_ref, counts_ref, blocks_ref, out_ref, sem):
    own = own_ref[0]
    upper = own >= n // 2
    add_count = lambda s, total: total + counts_ref[s]
    low = jnp.where(upper, own, 0)
    start = lax.fori_loop(low, jnp.where(upper, n, own), add_count, jnp.int32(0))
    start = jnp.where(upper, -start, start)
    copies = [
        pltpu.make_async_copy(blocks_ref.at[(d - start) & (n - 1)], out_ref.at[d], sem.at[d]) for d in range(n)
    ]
    for copy in copies:
        copy.start()
    for copy in copies:
        copy.wait()


def modes_kernel(n, slots, own_ref, counts_ref, recv_ref, inv_ref, out_ref, rows_ref, done_ref, sem):
    shift = n.bit_length() - 1
    own = own_ref[0]

    def place(s, start):
        first = start + ((own - start) & (n - 1))
        at = first >> shift
        turn = at & 7
        at = pl.multiple_of(at - turn, 8)
        block = pltpu.roll(jnp.concatenate([recv_ref[s], recv_ref[s, 0:8, :]], 0), turn, 0)
        head = lax.broadcasted_iota(jnp.int32, (8, block.shape[1]), 0) < turn
        rows_ref[pl.ds(at, 8), :] = jnp.where(head, rows_ref[pl.ds(at, 8), :], block[0:8])
        rows_ref[pl.ds(at + 8, slots), :] = block[8:]
        return start + counts_ref[s]

    lax.fori_loop(0, n, place, jnp.int32(0))
    step = out_ref.shape[0] // sem.shape[0]
    copies = []
    for c in range(sem.shape[0]):
        at = pl.ds(c * step, step)
        done_ref[at, :] = dot6(rows_ref[at, :], inv_ref[...], 1, 1)
        copies.append(pltpu.make_async_copy(done_ref.at[at], out_ref.at[at], sem.at[c]))
        copies[-1].start()
    for copy in copies:
        copy.wait()


VMEM = pl.BlockSpec(memory_space=pltpu.VMEM)
SMEM = pl.BlockSpec(memory_space=pltpu.SMEM)
HBM = pl.BlockSpec(memory_space=pltpu.HBM)


def call(kernel, name, out, in_specs, scratch, flops, args, out_space=VMEM):
    return pl.pallas_call(
        kernel,
        name=name,
        out_shape=out,
        in_specs=in_specs,
        out_specs=jax.tree.map(lambda _: out_space, out),
        scratch_shapes=scratch,
        compiler_params=pltpu.CompilerParams(vmem_limit_bytes=VMEM_LIMIT),
        cost_estimate=pl.CostEstimate(flops=flops, bytes_accessed=4 << 20, transcendentals=0),
    )(*args)


def other(x, bits, n):
    return lax.ppermute(x, "height", [(i, i ^ bits) for i in range(n)])


def add(a, b):
    return jnp.stack(add_pair(a, b))


def gather_quarters(mine, n):
    return [mine] + [other(mine, 2 * turn, n) for turn in (1, 2, 3)]


def assemble(got, own):
    place = (own >> 1) & 3
    return jnp.concatenate(
        [
            jnp.where(place < 2, *(jnp.where((place & 1) > 0, got[c ^ h ^ 1], got[c ^ h]) for h in (0, 2)))
            for c in range(4)
        ],
        1,
    )


def local(snapshots, fluid_mask):
    n = lax.axis_size("height")
    own = lax.axis_index("height")
    cells, k = snapshots.shape
    slots = (-(-MAXC // n) + 7) // 8 * 8
    own_list = own.reshape(1)
    mask = fluid_mask.reshape(cells // 128, 128)
    block = jnp.arange(cells // 128)
    starts = jnp.sum(jnp.where(block[None, :, None] < block[:, None, None], mask[None], 0), (1, 2))
    half = jax.ShapeDtypeStruct((2, 200, 128), F32)
    keep, send = call(
        functools.partial(gram_kernel, 1.0 / (n * BLK)),
        "gram",
        [half, half],
        [SMEM, VMEM, VMEM],
        [pltpu.VMEM((cells, k), F32)] + [pltpu.VMEM((cells, k), jnp.bfloat16)] * 4,
        16 * cells * k * k,
        (own_list, snapshots, mask),
    )
    size = keep.shape[1] // 4 // 8 * 8
    quarter = jax.ShapeDtypeStruct((2, size + 8, 128), F32)
    mine, side, up, across = call(
        quarter_kernel, "quarter", [quarter] * 4, [SMEM, VMEM, VMEM], [], 1 << 20, (own_list, keep, other(send, 1, n))
    )
    got = [other(across, 6, n), other(up, 4, n), other(side, 2, n)]
    starts, mine = lax.optimization_barrier((starts, mine))
    blocks = call(
        functools.partial(compact_kernel, n),
        "compact",
        jax.ShapeDtypeStruct((n, slots, k), F32),
        [SMEM, VMEM, VMEM],
        [pltpu.VMEM((cells // 128, 128), jnp.int32)],
        4 << 30,
        (starts, mask, snapshots),
    )
    got, blocks = lax.optimization_barrier((got, blocks))
    mine = add(add(mine, got[0]), add(got[1], got[2]))
    bit = 8
    while bit < n:
        near_counts = mine[0, size, :n].astype(jnp.int32)
        mine = add(mine, other(mine, bit, n))
        bit *= 2
    counts = mine[0, size, :n].astype(jnp.int32)
    quarters = gather_quarters(mine[:, :size], n)
    outgoing = call(
        functools.partial(turn_kernel, n),
        "turn",
        jax.ShapeDtypeStruct((n, slots, k), F32),
        [SMEM, SMEM, VMEM],
        [pltpu.SemaphoreType.DMA((n,))],
        1 << 20,
        (own_list, near_counts, blocks),
        out_space=HBM,
    )
    outgoing, counts = lax.optimization_barrier((outgoing, counts))
    received = lax.all_to_all(outgoing, "height", split_axis=0, concat_axis=0, tiled=True)
    half = assemble(quarters, own)
    got = other(half, 1, n)
    square = jax.ShapeDtypeStruct((k, k), F32)
    inverse, factor = call(
        chain_kernel,
        "chain",
        [square, square],
        [SMEM, VMEM, VMEM],
        [pltpu.VMEM((k, k), F32)] * 4,
        25 << 30,
        (own_list, half, got),
    )
    modes = call(
        functools.partial(modes_kernel, n, slots),
        "modes",
        jax.ShapeDtypeStruct((BLK, k), F32),
        [SMEM, SMEM, VMEM, VMEM],
        [pltpu.VMEM((BLK + slots + 8, k), F32), pltpu.VMEM((BLK, k), F32), pltpu.SemaphoreType.DMA((4,))],
        12 * BLK * k * k,
        (own_list, counts, received, inverse),
        out_space=HBM,
    )
    return (modes, factor)


def solution(mesh):
    return jax.shard_map(
        local,
        mesh=mesh,
        in_specs=(P(("parts", "height"), None), P(("parts", "height"))),
        out_specs=(P(("parts", "height"), None), P("parts", None)),
        check_vma=False,
    )
```

```python
import functools

import jax
import jax.numpy as jnp
from jax import lax
from jax.experimental import pallas as pl
from jax.experimental.pallas import tpu as pltpu
from jax.sharding import PartitionSpec as P

BLK = 1024
MAXC = 1536
F32 = jnp.float32
VMEM_LIMIT = 40 * 1024 * 1024


def split3(x):
    high = x.astype(jnp.bfloat16)
    rest = x - high.astype(F32)
    mid = rest.astype(jnp.bfloat16)
    return high, mid, (rest - mid.astype(F32)).astype(jnp.bfloat16)


def dot6(left, right, left_dim, right_dim):
    lh, lm, ll = split3(left)
    rh, rm, rl = split3(right)
    return lax.dot_general(
        jnp.concatenate([ll, lh, lm, lm, lh, lh], left_dim),
        jnp.concatenate([rh, rl, rm, rh, rm, rh], right_dim),
        (((left_dim,), (right_dim,)), ((), ())),
        preferred_element_type=F32,
    )


def two_sum(a, b):
    total = a + b
    part = total - a
    return total, (a - (total - part)) + (b - part)


def add_pair(a, b):
    total, error = two_sum(a[0], b[0])
    return total, (a[1] + b[1]) + error


def power_above(peak):
    power = jnp.full_like(peak, 2.0**-120)
    inverse = jnp.full_like(peak, 2.0**119)
    for step in (100, 64, 32, 16, 8, 4, 2, 1):
        trial = power * 2.0**step
        above = peak >= trial
        power = jnp.where(above, trial, power)
        inverse = jnp.where(above, inverse * 2.0**-step, inverse)
    return power * 2.0, inverse


def slices(x, bits):
    out = []
    for place in bits:
        big = 1.5 * 2.0 ** (23 - place)
        part = (x + big) - big
        out.append(part.astype(jnp.bfloat16))
        x = x - part
    part = x.astype(jnp.bfloat16)
    return out + [part, (x - part.astype(F32)).astype(jnp.bfloat16)]


def gram_pair(n1, n2, n3, n4, *n5):
    n = n1.shape[1]
    dims = (((0,), (0,)), ((), ()))
    d1 = lax.dot_general(n1, jnp.concatenate([n1, n2, n3, n4, *n5], 1), dims, preferred_element_type=F32)
    d2 = lax.dot_general(n2, jnp.concatenate([n2, n3, n4], 1), dims, preferred_element_type=F32)
    d3 = lax.dot_general(n3, n3, dims, preferred_element_type=F32)
    p11, p12, p13, p14 = (d1[:, i * n : (i + 1) * n] for i in range(4))
    p22, p23, p24 = (d2[:, i * n : (i + 1) * n] for i in range(3))
    hi, low1 = two_sum(p11, p12 + p12.T)
    hi, low2 = two_sum(hi, p22 + (p13 + p13.T))
    tail = p14 + p23 + p24
    if n5:
        tail = tail + d1[:, 4 * n :]
    return hi, (low1 + low2) + ((tail + tail.T) + d3)


def column_of(row):
    n = row.shape[1]
    return jnp.broadcast_to(row, (8, n)).T[:, 0:1]


def sweep(work, r_ref, w_ref, b=32, bi=8):
    n = work.shape[0]
    groups = b // 8
    lane = lax.broadcasted_iota(jnp.int32, (8, n), 1)
    sub_wide = lax.broadcasted_iota(jnp.int32, (8, n), 0)
    sub = lax.broadcasted_iota(jnp.int32, (8, 128), 0)

    def wide(x):
        return jnp.concatenate([x] * (n // 128), 1)

    for base in range(0, n, b):
        half = base // 128 * 128
        off = base - half
        own = (lane >= base) & (lane < base + b)
        rows, diag = [], []
        for g in range(groups):
            row = work[base + 8 * g : base + 8 * g + 8, :]
            diag.append(row[:, half : half + 128])
            rows.append(jnp.where(own, jnp.where(lane == base + 8 * g + sub_wide, 1.0, 0.0), row))
        pivots = [jnp.ones((8, 128), F32)] * groups
        for k0 in range(0, b, bi):
            col = {}
            for kk in range(bi):
                for g in range(k0 // 8, groups):
                    at = off + k0 + kk
                    col[kk, g] = jnp.broadcast_to(diag[g][:, at : at + 1], (8, 128))
            for kk in range(bi):
                own_group, s = divmod(k0 + kk, 8)
                pivot = jnp.broadcast_to(col[kk, own_group][s : s + 1, :], (8, 128))
                inverse = 1.0 / pivot
                pivots[own_group] = jnp.where(sub == s, pivot, pivots[own_group])
                mult = {}
                for g in range(own_group, groups):
                    value = col[kk, g] * inverse
                    mult[g] = jnp.where(sub > s, value, 0.0) if g == own_group else value
                for k2 in range(kk + 1, bi):
                    entry = jnp.broadcast_to(col[k2, own_group][s : s + 1, :], (8, 128))
                    for g in range(own_group, groups):
                        col[k2, g] = col[k2, g] - mult[g] * entry
                pivot_row = jnp.broadcast_to(rows[own_group][s : s + 1, :], (8, n))
                pivot_diag = jnp.broadcast_to(diag[own_group][s : s + 1, :], (8, 128))
                for g in range(own_group, groups):
                    rows[g] = rows[g] - wide(mult[g]) * pivot_row
                    diag[g] = diag[g] - mult[g] * pivot_diag
        right, full = [], []
        for g in range(groups):
            scale = lax.rsqrt(pivots[g])
            scale = scale + scale * (0.5 - (0.5 * pivots[g]) * scale * scale)
            scaled = rows[g] * wide(scale)
            own_diag = diag[g] * scale
            blocks = [own_diag if h == half else jnp.zeros((8, 128), F32) for h in range(0, n, 128)]
            upper = own & (lane >= base + 8 * g + sub_wide)
            after = jnp.where(lane >= base + b, scaled, 0.0)
            r_ref[base + 8 * g : base + 8 * g + 8, :] = jnp.where(upper, jnp.concatenate(blocks, 1), after)
            w_ref[base + 8 * g : base + 8 * g + 8, :] = jnp.where(lane < base + b, scaled, 0.0)
            right.append(after)
            full.append(scaled)
        if base + b < n:
            low = (base + b) // 128 * 128
            update = dot6(jnp.concatenate(right, 0)[:, low:], jnp.concatenate(full, 0), 0, 0)
            lanes = lax.broadcasted_iota(jnp.int32, (n - low, n), 1)
            tail = jnp.where((lanes >= base) & (lanes < base + b), 0.0, work[low:, :]) - update
            work = tail if low == 0 else jnp.concatenate([jnp.zeros((low, n), F32), tail], 0)


def block_upper(matrix, b=32):
    n = matrix.shape[0]
    row = lax.broadcasted_iota(jnp.int32, (n, n), 0) // b
    column = lax.broadcasted_iota(jnp.int32, (n, n), 1) // b
    return jnp.where(column < row, 0.0, matrix)


def gram_kernel(row_scale, own_ref, x_ref, mask_ref, keep_ref, send_ref, a_ref, n1_ref, n2_ref, n3_ref, n4_ref):
    rows, n = x_ref.shape
    peak = jnp.zeros((8, n), F32)
    for c in range(rows // 128):
        keep = jnp.broadcast_to(mask_ref[c : c + 1, :], (128, 128)).T
        keep = jnp.concatenate([keep] * (n // 128), 1)
        chunk = jnp.where(keep > 0, x_ref[c * 128 : c * 128 + 128, :], 0.0)
        a_ref[c * 128 : c * 128 + 128, :] = chunk
        peak = jnp.maximum(peak, jnp.max(jnp.abs(chunk).reshape(16, 8, n), axis=0))
    top, shrink = power_above(jnp.max(peak, axis=0, keepdims=True))
    for c in range(rows // 128):
        at = slice(c * 128, c * 128 + 128)
        for ref, part in zip((n1_ref, n2_ref, n3_ref, n4_ref), slices(a_ref[at, :] * shrink, (6, 14, 22))):
            ref[at, :] = part
    pair = gram_pair(n1_ref[...], n2_ref[...], n3_ref[...], n4_ref[...])
    column, grow = column_of(top), top * row_scale
    odd = (own_ref[0] & 1) > 0
    live = jnp.sum(mask_ref[...].astype(F32), axis=(0, 1), keepdims=True)
    lane = lax.broadcasted_iota(jnp.int32, (8, 128), 1)
    row = lax.broadcasted_iota(jnp.int32, (8, 128), 0)
    count = jnp.where((lane == own_ref[0]) & (row == 0), live, 0.0)
    for index, value in enumerate(pair):
        value = value * column * grow
        last = value[128:256, 128:256]
        first = value[0:128, 128:256]
        second = jnp.where(upper_half(), value[0:128, 0:128], last)
        extra = jnp.sum(jnp.where(diagonal(), last, 0.0), axis=0, keepdims=True)
        extra = jnp.where(row == 1, extra, count if index == 0 else 0.0)
        size = first.shape[0]
        keep_ref[index, 0:size] = jnp.where(odd, second, first)
        send_ref[index, 0:size] = jnp.where(odd, first, second)
        for ref in (keep_ref, send_ref):
            ref[index, size:] = extra


def quarter_kernel(own_ref, keep_ref, got_ref, mine_ref, send_ref):
    size = mine_ref.shape[1] - 8
    place = (own_ref[0] >> 1) & 1
    for turn, ref in enumerate((mine_ref, send_ref)):
        for to, at in (
            (pl.ds(0, size), pl.ds(pl.multiple_of((place ^ turn) * size, 8), size)),
            (pl.ds(size, 8), pl.ds(2 * size, 8)),
        ):
            ref[0, to, :], ref[1, to, :] = add_pair(
                (keep_ref[0, at, :], keep_ref[1, at, :]), (got_ref[0, at, :], got_ref[1, at, :])
            )


def upper_half():
    return lax.broadcasted_iota(jnp.int32, (128, 128), 0) <= lax.broadcasted_iota(jnp.int32, (128, 128), 1)


def diagonal():
    return lax.broadcasted_iota(jnp.int32, (128, 128), 0) == lax.broadcasted_iota(jnp.int32, (128, 128), 1)


def unpack(right, mixed, extra):
    upper = jnp.where(upper_half(), mixed, 0.0)
    lower = mixed - upper
    first = upper + jnp.where(diagonal(), 0.0, upper).T
    last = lower + lower.T + jnp.where(diagonal(), extra, 0.0)
    return jnp.concatenate([jnp.concatenate([first, right], 1), jnp.concatenate([right.T, last], 1)], 0)


def chain_kernel(own_ref, half_ref, got_ref, extra_ref, inv_ref, factor_ref, r1, w1, r2, w2):
    odd = (own_ref[0] & 1) > 0
    hi, lo = (
        unpack(jnp.where(odd, got_ref[i], half_ref[i]), jnp.where(odd, half_ref[i], got_ref[i]), extra_ref[i, 1:2, :])
        for i in range(2)
    )
    sweep(block_upper(hi), r1, w1)
    r = r1[...]
    top, shrink = power_above(jnp.max(jnp.abs(r), axis=0, keepdims=True))
    own_hi, own_lo = gram_pair(*slices(r * shrink, (7, 15, 23)))
    column = column_of(top)
    residual = (hi - own_hi * column * top) + (lo - own_lo * column * top)
    w = w1[...]
    near = dot6(w, r, 1, 1)
    gram2 = dot6(near, near, 1, 1) + dot6(dot6(w, residual, 1, 0), w, 1, 1)
    sweep(block_upper(gram2), r2, w2)
    row = lax.broadcasted_iota(jnp.int32, near.shape, 0)
    twice = jnp.where(row == lax.broadcasted_iota(jnp.int32, near.shape, 1), 2.0, 0.0)
    factor_ref[...] = dot6(r2[...], dot6(twice - near, r, 0, 0), 1, 0)
    inv_ref[...] = dot6(w2[...], w, 1, 0)


def compact_kernel(n, starts_ref, mask_ref, x_ref, out_ref, rank_ref):
    slots = out_ref.shape[1]
    shift = n.bit_length() - 1
    width = 16
    blocks = mask_ref.shape[0]
    live = mask_ref[...]
    before = lax.broadcasted_iota(jnp.int32, (128, 128), 0) < lax.broadcasted_iota(jnp.int32, (128, 128), 1)
    rank_ref[...] = jnp.dot(
        live.astype(F32).astype(jnp.bfloat16),
        jnp.where(before, 1.0, 0.0).astype(jnp.bfloat16),
        preferred_element_type=F32,
    ).astype(jnp.int32)
    out_ref[...] = jnp.zeros_like(out_ref)
    row = lax.broadcasted_iota(jnp.int32, (n * width, 128), 0)

    def step(b, _):
        first = starts_ref[b]
        low = pl.multiple_of(jnp.minimum((first >> shift) & -8, slots - width), 8)
        rank = rank_ref[pl.ds(b, 1), :] + first
        target = (rank & (n - 1)) * width + (rank >> shift) - low
        target = jnp.where(mask_ref[pl.ds(b, 1), :] > 0, target, -1)
        pick = jnp.where(row == target, 1.0, 0.0).astype(jnp.bfloat16)
        cells = x_ref[pl.ds(pl.multiple_of(b * 128, 128), 128), :]
        moved = jnp.dot(
            jnp.concatenate([pick] * 3, 1), jnp.concatenate(split3(cells), 0), preferred_element_type=F32
        )
        for c in range(n):
            out_ref[c, pl.ds(low, width), :] += moved[c * width : c * width + width]
        return 0

    lax.fori_loop(0, blocks, step, 0, unroll=4 if n <= 16 else 1)


def turn_kernel(n, own_ref, counts_ref, blocks_ref, out_ref, sem):
    own = own_ref[0]
    upper = own >= n // 2
    add_count = lambda s, total: total + counts_ref[s]
    low = jnp.where(upper, own, 0)
    start = lax.fori_loop(low, jnp.where(upper, n, own), add_count, jnp.int32(0))
    start = jnp.where(upper, -start, start)
    copies = [
        pltpu.make_async_copy(blocks_ref.at[(d - start) & (n - 1)], out_ref.at[d], sem.at[d]) for d in range(n)
    ]
    for copy in copies:
        copy.start()
    for copy in copies:
        copy.wait()


def modes_kernel(n, slots, own_ref, counts_ref, recv_ref, inv_ref, out_ref, rows_ref, done_ref, sem):
    shift = n.bit_length() - 1
    own = own_ref[0]

    def place(s, start):
        first = start + ((own - start) & (n - 1))
        at = first >> shift
        turn = at & 7
        at = pl.multiple_of(at - turn, 8)
        block = pltpu.roll(jnp.concatenate([recv_ref[s], recv_ref[s, 0:8, :]], 0), turn, 0)
        head = lax.broadcasted_iota(jnp.int32, (8, block.shape[1]), 0) < turn
        rows_ref[pl.ds(at, 8), :] = jnp.where(head, rows_ref[pl.ds(at, 8), :], block[0:8])
        rows_ref[pl.ds(at + 8, slots), :] = block[8:]
        return start + counts_ref[s]

    lax.fori_loop(0, n, place, jnp.int32(0))
    step = out_ref.shape[0] // sem.shape[0]
    copies = []
    for c in range(sem.shape[0]):
        at = pl.ds(c * step, step)
        done_ref[at, :] = dot6(rows_ref[at, :], inv_ref[...], 1, 1)
        copies.append(pltpu.make_async_copy(done_ref.at[at], out_ref.at[at], sem.at[c]))
        copies[-1].start()
    for copy in copies:
        copy.wait()


VMEM = pl.BlockSpec(memory_space=pltpu.VMEM)
SMEM = pl.BlockSpec(memory_space=pltpu.SMEM)
HBM = pl.BlockSpec(memory_space=pltpu.HBM)


def call(kernel, name, out, in_specs, scratch, flops, args, out_space=VMEM):
    return pl.pallas_call(
        kernel,
        name=name,
        out_shape=out,
        in_specs=in_specs,
        out_specs=jax.tree.map(lambda _: out_space, out),
        scratch_shapes=scratch,
        compiler_params=pltpu.CompilerParams(vmem_limit_bytes=VMEM_LIMIT),
        cost_estimate=pl.CostEstimate(flops=flops, bytes_accessed=4 << 20, transcendentals=0),
    )(*args)


def other(x, bits, n):
    return lax.ppermute(x, "height", [(i, i ^ bits) for i in range(n)])


def add(a, b):
    return jnp.stack(add_pair(a, b))


def local(snapshots, fluid_mask):
    n = lax.axis_size("height")
    own = lax.axis_index("height")
    cells, k = snapshots.shape
    slots = (-(-MAXC // n) + 7) // 8 * 8
    own_list = own.reshape(1)
    mask = fluid_mask.reshape(cells // 128, 128)
    block = jnp.arange(cells // 128)
    starts = jnp.sum(jnp.where(block[None, :, None] < block[:, None, None], mask[None], 0), (1, 2))
    half = jax.ShapeDtypeStruct((2, 136, 128), F32)
    keep, send = call(
        functools.partial(gram_kernel, 1.0 / (n * BLK)),
        "gram",
        [half, half],
        [SMEM, VMEM, VMEM],
        [pltpu.VMEM((cells, k), F32)] + [pltpu.VMEM((cells, k), jnp.bfloat16)] * 4,
        16 * cells * k * k,
        (own_list, snapshots, mask),
    )
    size = (keep.shape[1] - 8) // 2
    quarter = jax.ShapeDtypeStruct((2, size + 8, 128), F32)
    mine, sent = call(
        quarter_kernel, "quarter", [quarter] * 2, [SMEM, VMEM, VMEM], [], 1 << 20, (own_list, keep, other(send, 1, n))
    )
    got = other(sent, 2, n)
    starts, mine = lax.optimization_barrier((starts, mine))
    blocks = call(
        functools.partial(compact_kernel, n),
        "compact",
        jax.ShapeDtypeStruct((n, slots, k), F32),
        [SMEM, VMEM, VMEM],
        [pltpu.VMEM((cells // 128, 128), jnp.int32)],
        4 << 30,
        (starts, mask, snapshots),
    )
    got, blocks = lax.optimization_barrier((got, blocks))
    mine = add(mine, got)
    bit = 4
    while bit < n:
        near_counts = mine[0, size, :n].astype(jnp.int32)
        mine = add(mine, other(mine, bit, n))
        bit *= 2
    counts = mine[0, size, :n].astype(jnp.int32)
    extra = mine[:, size:]
    mine = mine[:, :size]
    outgoing = call(
        functools.partial(turn_kernel, n),
        "turn",
        jax.ShapeDtypeStruct((n, slots, k), F32),
        [SMEM, SMEM, VMEM],
        [pltpu.SemaphoreType.DMA((n,))],
        1 << 20,
        (own_list, near_counts, blocks),
        out_space=HBM,
    )
    received = lax.all_to_all(outgoing, "height", split_axis=0, concat_axis=0, tiled=True)
    got = other(mine, 2, n)
    high = (own & 2) > 0
    half = jnp.concatenate([jnp.where(high, got, mine), jnp.where(high, mine, got)], 1)
    got = other(half, 1, n)
    square = jax.ShapeDtypeStruct((k, k), F32)
    inverse, factor = call(
        chain_kernel,
        "chain",
        [square, square],
        [SMEM, VMEM, VMEM, VMEM],
        [pltpu.VMEM((k, k), F32)] * 4,
        20 << 30,
        (own_list, half, got, extra),
    )
    modes = call(
        functools.partial(modes_kernel, n, slots),
        "modes",
        jax.ShapeDtypeStruct((BLK, k), F32),
        [SMEM, SMEM, VMEM, VMEM],
        [pltpu.VMEM((BLK + slots + 8, k), F32), pltpu.VMEM((BLK, k), F32), pltpu.SemaphoreType.DMA((4,))],
        12 * BLK * k * k,
        (own_list, counts, received, inverse),
        out_space=HBM,
    )
    return (modes, factor)


def solution(mesh):
    return jax.shard_map(
        local,
        mesh=mesh,
        in_specs=(P(("parts", "height"), None), P(("parts", "height"))),
        out_specs=(P(("parts", "height"), None), P("parts", None)),
        check_vma=False,
    )
```

```python
import functools

import jax
import jax.numpy as jnp
from jax import lax
from jax.experimental import pallas as pl
from jax.experimental.pallas import tpu as pltpu
from jax.sharding import PartitionSpec as P

BLK = 1024
MAXC = 1536
F32 = jnp.float32
VMEM_LIMIT = 40 * 1024 * 1024


def split3(x):
    high = x.astype(jnp.bfloat16)
    rest = x - high.astype(F32)
    mid = rest.astype(jnp.bfloat16)
    return high, mid, (rest - mid.astype(F32)).astype(jnp.bfloat16)


def dot6(left, right, left_dim, right_dim):
    lh, lm, ll = split3(left)
    rh, rm, rl = split3(right)
    return lax.dot_general(
        jnp.concatenate([ll, lh, lm, lm, lh, lh], left_dim),
        jnp.concatenate([rh, rl, rm, rh, rm, rh], right_dim),
        (((left_dim,), (right_dim,)), ((), ())),
        preferred_element_type=F32,
    )


def two_sum(a, b):
    total = a + b
    part = total - a
    return total, (a - (total - part)) + (b - part)


def add_pair(a, b):
    total, error = two_sum(a[0], b[0])
    return total, (a[1] + b[1]) + error


def power_above(peak):
    power = jnp.full_like(peak, 2.0**-120)
    inverse = jnp.full_like(peak, 2.0**119)
    for step in (100, 64, 32, 16, 8, 4, 2, 1):
        trial = power * 2.0**step
        above = peak >= trial
        power = jnp.where(above, trial, power)
        inverse = jnp.where(above, inverse * 2.0**-step, inverse)
    return power * 2.0, inverse


def slices(x, bits):
    out = []
    for place in bits:
        big = 1.5 * 2.0 ** (23 - place)
        part = (x + big) - big
        out.append(part.astype(jnp.bfloat16))
        x = x - part
    part = x.astype(jnp.bfloat16)
    return out + [part, (x - part.astype(F32)).astype(jnp.bfloat16)]


def gram_pair(n1, n2, n3, n4, *n5):
    n = n1.shape[1]
    dims = (((0,), (0,)), ((), ()))
    d1 = lax.dot_general(n1, jnp.concatenate([n1, n2, n3, n4, *n5], 1), dims, preferred_element_type=F32)
    d2 = lax.dot_general(n2, jnp.concatenate([n2, n3, n4], 1), dims, preferred_element_type=F32)
    d3 = lax.dot_general(n3, n3, dims, preferred_element_type=F32)
    p11, p12, p13, p14 = (d1[:, i * n : (i + 1) * n] for i in range(4))
    p22, p23, p24 = (d2[:, i * n : (i + 1) * n] for i in range(3))
    hi, low1 = two_sum(p11, p12 + p12.T)
    hi, low2 = two_sum(hi, p22 + (p13 + p13.T))
    tail = p14 + p23 + p24
    if n5:
        tail = tail + d1[:, 4 * n :]
    return hi, (low1 + low2) + ((tail + tail.T) + d3)


def column_of(row):
    n = row.shape[1]
    return jnp.broadcast_to(row, (8, n)).T[:, 0:1]


def sweep(work, r_ref, w_ref, b=32, bi=16):
    n = work.shape[0]
    groups = b // 8
    lane = lax.broadcasted_iota(jnp.int32, (8, n), 1)
    sub_wide = lax.broadcasted_iota(jnp.int32, (8, n), 0)
    sub = lax.broadcasted_iota(jnp.int32, (8, 128), 0)

    def wide(x):
        return jnp.concatenate([x] * (n // 128), 1)

    for base in range(0, n, b):
        half = base // 128 * 128
        off = base - half
        own = (lane >= base) & (lane < base + b)
        rows, diag = [], []
        for g in range(groups):
            row = work[base + 8 * g : base + 8 * g + 8, :]
            diag.append(row[:, half : half + 128])
            rows.append(jnp.where(own, jnp.where(lane == base + 8 * g + sub_wide, 1.0, 0.0), row))
        pivots = [jnp.ones((8, 128), F32)] * groups
        for k0 in range(0, b, bi):
            col = {}
            for kk in range(bi):
                for g in range(k0 // 8, groups):
                    at = off + k0 + kk
                    col[kk, g] = jnp.broadcast_to(diag[g][:, at : at + 1], (8, 128))
            for kk in range(bi):
                own_group, s = divmod(k0 + kk, 8)
                pivot = jnp.broadcast_to(col[kk, own_group][s : s + 1, :], (8, 128))
                inverse = 1.0 / pivot
                pivots[own_group] = jnp.where(sub == s, pivot, pivots[own_group])
                mult = {}
                for g in range(own_group, groups):
                    value = col[kk, g] * inverse
                    mult[g] = jnp.where(sub > s, value, 0.0) if g == own_group else value
                for k2 in range(kk + 1, bi):
                    entry = jnp.broadcast_to(col[k2, own_group][s : s + 1, :], (8, 128))
                    for g in range(own_group, groups):
                        if k2 == kk + 1:
                            col[k2, g] = col[k2, g] - (col[kk, g] * entry) * inverse
                        else:
                            col[k2, g] = col[k2, g] - mult[g] * entry
                pivot_row = jnp.broadcast_to(rows[own_group][s : s + 1, :], (8, n))
                pivot_diag = jnp.broadcast_to(diag[own_group][s : s + 1, :], (8, 128))
                for g in range(own_group, groups):
                    rows[g] = rows[g] - wide(mult[g]) * pivot_row
                    diag[g] = diag[g] - mult[g] * pivot_diag
        right, full = [], []
        for g in range(groups):
            scale = lax.rsqrt(pivots[g])
            scale = scale + scale * (0.5 - (0.5 * pivots[g]) * scale * scale)
            scaled = rows[g] * wide(scale)
            own_diag = diag[g] * scale
            blocks = [own_diag if h == half else jnp.zeros((8, 128), F32) for h in range(0, n, 128)]
            upper = own & (lane >= base + 8 * g + sub_wide)
            after = jnp.where(lane >= base + b, scaled, 0.0)
            r_ref[base + 8 * g : base + 8 * g + 8, :] = jnp.where(upper, jnp.concatenate(blocks, 1), after)
            w_ref[base + 8 * g : base + 8 * g + 8, :] = jnp.where(lane < base + b, scaled, 0.0)
            right.append(after)
            full.append(scaled)
        if base + b < n:
            low = (base + b) // 128 * 128
            update = dot6(jnp.concatenate(right, 0)[:, low:], jnp.concatenate(full, 0), 0, 0)
            lanes = lax.broadcasted_iota(jnp.int32, (n - low, n), 1)
            tail = jnp.where((lanes >= base) & (lanes < base + b), 0.0, work[low:, :]) - update
            work = tail if low == 0 else jnp.concatenate([jnp.zeros((low, n), F32), tail], 0)


def block_upper(matrix, b=32):
    n = matrix.shape[0]
    row = lax.broadcasted_iota(jnp.int32, (n, n), 0) // b
    column = lax.broadcasted_iota(jnp.int32, (n, n), 1) // b
    return jnp.where(column < row, 0.0, matrix)


def gram_kernel(row_scale, own_ref, x_ref, mask_ref, mine_ref, core_ref, side_ref, both_ref, a_ref, n1_ref, n2_ref, n3_ref, n4_ref):
    rows, n = x_ref.shape
    peak = jnp.zeros((8, n), F32)
    for c in range(rows // 128):
        keep = jnp.broadcast_to(mask_ref[c : c + 1, :], (128, 128)).T
        keep = jnp.concatenate([keep] * (n // 128), 1)
        chunk = jnp.where(keep > 0, x_ref[c * 128 : c * 128 + 128, :], 0.0)
        a_ref[c * 128 : c * 128 + 128, :] = chunk
        peak = jnp.maximum(peak, jnp.max(jnp.abs(chunk).reshape(16, 8, n), axis=0))
    top, shrink = power_above(jnp.max(peak, axis=0, keepdims=True))
    for c in range(rows // 128):
        at = slice(c * 128, c * 128 + 128)
        for ref, part in zip((n1_ref, n2_ref, n3_ref, n4_ref), slices(a_ref[at, :] * shrink, (6, 14, 22))):
            ref[at, :] = part
    pair = gram_pair(n1_ref[...], n2_ref[...], n3_ref[...], n4_ref[...])
    column, grow = column_of(top), top * row_scale
    refs = (mine_ref, core_ref, side_ref, both_ref)
    live = jnp.sum(mask_ref[...].astype(F32), axis=(0, 1), keepdims=True)
    lane = lax.broadcasted_iota(jnp.int32, (8, 128), 1)
    row = lax.broadcasted_iota(jnp.int32, (8, 128), 0)
    count = jnp.where((lane == own_ref[0]) & (row == 0), live, 0.0)
    for index, value in enumerate(pair):
        value = value * column * grow
        last = value[128:256, 128:256]
        first = value[0:128, 128:256]
        second = jnp.where(upper_half(), value[0:128, 0:128], last)
        extra = jnp.sum(jnp.where(diagonal(), last, 0.0), axis=0, keepdims=True)
        extra = jnp.where(row == 1, extra, count if index == 0 else 0.0)
        size = first.shape[0] // 2
        for turn, ref in enumerate(refs):
            place = own_ref[0] ^ turn
            block = jnp.where((place & 1) > 0, second, first)
            ref[index, 0:size] = jnp.where((place & 2) > 0, block[size:], block[:size])
            ref[index, size:] = extra


def upper_half():
    return lax.broadcasted_iota(jnp.int32, (128, 128), 0) <= lax.broadcasted_iota(jnp.int32, (128, 128), 1)


def diagonal():
    return lax.broadcasted_iota(jnp.int32, (128, 128), 0) == lax.broadcasted_iota(jnp.int32, (128, 128), 1)


def unpack(right, mixed, extra):
    upper = jnp.where(upper_half(), mixed, 0.0)
    lower = mixed - upper
    first = upper + jnp.where(diagonal(), 0.0, upper).T
    last = lower + lower.T + jnp.where(diagonal(), extra, 0.0)
    return jnp.concatenate([jnp.concatenate([first, right], 1), jnp.concatenate([right.T, last], 1)], 0)


def chain_kernel(own_ref, half_ref, got_ref, extra_ref, inv_ref, factor_ref, r1, w1, r2, w2):
    odd = (own_ref[0] & 1) > 0
    hi, lo = (
        unpack(jnp.where(odd, got_ref[i], half_ref[i]), jnp.where(odd, half_ref[i], got_ref[i]), extra_ref[i, 1:2, :])
        for i in range(2)
    )
    sweep(block_upper(hi), r1, w1)
    r = r1[...]
    top, shrink = power_above(jnp.max(jnp.abs(r), axis=0, keepdims=True))
    own_hi, own_lo = gram_pair(*slices(r * shrink, (7, 15, 23)))
    column = column_of(top)
    residual = (hi - own_hi * column * top) + (lo - own_lo * column * top)
    w = w1[...]
    near = dot6(w, r, 1, 1)
    gram2 = dot6(near, near, 1, 1) + dot6(dot6(w, residual, 1, 0), w, 1, 1)
    sweep(block_upper(gram2), r2, w2)
    row = lax.broadcasted_iota(jnp.int32, near.shape, 0)
    twice = jnp.where(row == lax.broadcasted_iota(jnp.int32, near.shape, 1), 2.0, 0.0)
    factor_ref[...] = dot6(r2[...], dot6(twice - near, r, 0, 0), 1, 0)
    inv_ref[...] = dot6(w2[...], w, 1, 0)


def compact_kernel(n, starts_ref, mask_ref, x_ref, out_ref, rank_ref):
    slots = out_ref.shape[1]
    shift = n.bit_length() - 1
    width = 16
    blocks = mask_ref.shape[0]
    live = mask_ref[...]
    before = lax.broadcasted_iota(jnp.int32, (128, 128), 0) < lax.broadcasted_iota(jnp.int32, (128, 128), 1)
    rank_ref[...] = jnp.dot(
        live.astype(F32).astype(jnp.bfloat16),
        jnp.where(before, 1.0, 0.0).astype(jnp.bfloat16),
        preferred_element_type=F32,
    ).astype(jnp.int32)
    out_ref[...] = jnp.zeros_like(out_ref)
    row = lax.broadcasted_iota(jnp.int32, (n * width, 128), 0)

    def step(b, _):
        first = starts_ref[b]
        low = pl.multiple_of(jnp.minimum((first >> shift) & -8, slots - width), 8)
        rank = rank_ref[pl.ds(b, 1), :] + first
        target = (rank & (n - 1)) * width + (rank >> shift) - low
        target = jnp.where(mask_ref[pl.ds(b, 1), :] > 0, target, -1)
        pick = jnp.where(row == target, 1.0, 0.0).astype(jnp.bfloat16)
        cells = x_ref[pl.ds(pl.multiple_of(b * 128, 128), 128), :]
        moved = jnp.dot(
            jnp.concatenate([pick] * 3, 1), jnp.concatenate(split3(cells), 0), preferred_element_type=F32
        )
        for c in range(n):
            out_ref[c, pl.ds(low, width), :] += moved[c * width : c * width + width]
        return 0

    lax.fori_loop(0, blocks, step, 0, unroll=4 if n <= 16 else 1)


def turn_kernel(n, own_ref, counts_ref, blocks_ref, out_ref, sem):
    own = own_ref[0]
    upper = own >= n // 2
    add_count = lambda s, total: total + counts_ref[s]
    low = jnp.where(upper, own, 0)
    start = lax.fori_loop(low, jnp.where(upper, n, own), add_count, jnp.int32(0))
    start = jnp.where(upper, -start, start)
    copies = [
        pltpu.make_async_copy(blocks_ref.at[(d - start) & (n - 1)], out_ref.at[d], sem.at[d]) for d in range(n)
    ]
    for copy in copies:
        copy.start()
    for copy in copies:
        copy.wait()


def modes_kernel(n, slots, own_ref, counts_ref, recv_ref, inv_ref, out_ref, rows_ref, done_ref, sem):
    shift = n.bit_length() - 1
    own = own_ref[0]

    def place(s, start):
        first = start + ((own - start) & (n - 1))
        at = first >> shift
        turn = at & 7
        at = pl.multiple_of(at - turn, 8)
        block = pltpu.roll(jnp.concatenate([recv_ref[s], recv_ref[s, 0:8, :]], 0), turn, 0)
        head = lax.broadcasted_iota(jnp.int32, (8, block.shape[1]), 0) < turn
        rows_ref[pl.ds(at, 8), :] = jnp.where(head, rows_ref[pl.ds(at, 8), :], block[0:8])
        rows_ref[pl.ds(at + 8, slots), :] = block[8:]
        return start + counts_ref[s]

    lax.fori_loop(0, n, place, jnp.int32(0), unroll=4)
    step = out_ref.shape[0] // sem.shape[0]
    copies = []
    for c in range(sem.shape[0]):
        at = pl.ds(c * step, step)
        done_ref[at, :] = lax.dot_general(
            rows_ref[at, :],
            inv_ref[...],
            (((1,), (1,)), ((), ())),
            precision=lax.Precision.HIGHEST,
            preferred_element_type=F32,
        )
        copies.append(pltpu.make_async_copy(done_ref.at[at], out_ref.at[at], sem.at[c]))
        copies[-1].start()
    for copy in copies:
        copy.wait()


VMEM = pl.BlockSpec(memory_space=pltpu.VMEM)
SMEM = pl.BlockSpec(memory_space=pltpu.SMEM)
HBM = pl.BlockSpec(memory_space=pltpu.HBM)


def call(kernel, name, out, in_specs, scratch, flops, args, out_space=VMEM):
    return pl.pallas_call(
        kernel,
        name=name,
        out_shape=out,
        in_specs=in_specs,
        out_specs=jax.tree.map(lambda _: out_space, out),
        scratch_shapes=scratch,
        compiler_params=pltpu.CompilerParams(vmem_limit_bytes=VMEM_LIMIT),
        cost_estimate=pl.CostEstimate(flops=flops, bytes_accessed=4 << 20, transcendentals=0),
    )(*args)


def other(x, bits, n):
    return lax.ppermute(x, "height", [(i, i ^ bits) for i in range(n)])


def add(a, b):
    return jnp.stack(add_pair(a, b))


def local(snapshots, fluid_mask):
    n = lax.axis_size("height")
    own = lax.axis_index("height")
    cells, k = snapshots.shape
    slots = (-(-MAXC // n) + 7) // 8 * 8
    own_list = own.reshape(1)
    mask = fluid_mask.reshape(cells // 128, 128)
    block = jnp.arange(cells // 128)
    starts = jnp.sum(jnp.where(block[None, :, None] < block[:, None, None], mask[None], 0), (1, 2))
    size = 64
    quarter = jax.ShapeDtypeStruct((2, size + 8, 128), F32)
    mine, *sent = call(
        functools.partial(gram_kernel, 1.0 / (n * BLK)),
        "gram",
        [quarter] * 4,
        [SMEM, VMEM, VMEM],
        [pltpu.VMEM((cells, k), F32)] + [pltpu.VMEM((cells, k), jnp.bfloat16)] * 4,
        16 * cells * k * k,
        (own_list, snapshots, mask),
    )
    got = [other(x, turn, n) for turn, x in zip((3, 2, 1), sent[::-1])]
    mine = add(add(mine, got[2]), add(got[1], got[0]))
    starts, mine = lax.optimization_barrier((starts, mine))
    blocks = call(
        functools.partial(compact_kernel, n),
        "compact",
        jax.ShapeDtypeStruct((n, slots, k), F32),
        [SMEM, VMEM, VMEM],
        [pltpu.VMEM((cells // 128, 128), jnp.int32)],
        4 << 30,
        (starts, mask, snapshots),
    )
    bit = 4
    while bit < n:
        near_counts = mine[0, size, :n].astype(jnp.int32)
        got = other(mine, bit, n)
        if bit == 4:
            got, blocks = lax.optimization_barrier((got, blocks))
        mine = add(mine, got)
        bit *= 2
    counts = mine[0, size, :n].astype(jnp.int32)
    extra = mine[:, size:]
    mine = mine[:, :size]
    outgoing = call(
        functools.partial(turn_kernel, n),
        "turn",
        jax.ShapeDtypeStruct((n, slots, k), F32),
        [SMEM, SMEM, VMEM],
        [pltpu.SemaphoreType.DMA((n,))],
        1 << 20,
        (own_list, near_counts, blocks),
        out_space=HBM,
    )
    received = lax.all_to_all(outgoing, "height", split_axis=0, concat_axis=0, tiled=True)
    got = other(mine, 2, n)
    high = (own & 2) > 0
    half = jnp.concatenate([jnp.where(high, got, mine), jnp.where(high, mine, got)], 1)
    got = other(half, 1, n)
    square = jax.ShapeDtypeStruct((k, k), F32)
    inverse, factor = call(
        chain_kernel,
        "chain",
        [square, square],
        [SMEM, VMEM, VMEM, VMEM],
        [pltpu.VMEM((k, k), F32)] * 4,
        20 << 30,
        (own_list, half, got, extra),
    )
    modes = call(
        functools.partial(modes_kernel, n, slots),
        "modes",
        jax.ShapeDtypeStruct((BLK, k), F32),
        [SMEM, SMEM, VMEM, VMEM],
        [pltpu.VMEM((BLK + slots + 8, k), F32), pltpu.VMEM((BLK, k), F32), pltpu.SemaphoreType.DMA((4,))],
        12 * BLK * k * k,
        (own_list, counts, received, inverse),
        out_space=HBM,
    )
    return (modes, factor)


def solution(mesh):
    return jax.shard_map(
        local,
        mesh=mesh,
        in_specs=(P(("parts", "height"), None), P(("parts", "height"))),
        out_specs=(P(("parts", "height"), None), P("parts", None)),
        check_vma=False,
    )
```
